32 devices in a mesh: grp: 2 (over x), ty: 16 (over z, y, core).
Axes of the slice: x: 2, y: 2, z: 4, core: 2. Of those that a mesh axis runs over, the one named last changes fastest.
Arguments:
- tile_object: float32 [4, 2, 4096, 768], P(None, None, ('grp', 'ty')), parts along dimension 2, may hold values from -6 to 6
- probe_wave: float32 [2, 128, 128], replicated, may hold values from -6 to 6
- propagator_phase: float32 [128, 128], replicated, may hold values from -3.140625 to 3.140625
- diffraction: float32 [128, 128, 128], P(('grp', 'ty')), parts along dimension 0, may hold values from 0 to 2
- positions: int32 [128, 2], P(('grp', 'ty')), parts along dimension 0, may hold values from 0 to 640, as said below
- counts: int32 [32], P(('grp', 'ty')), parts along dimension 0, may hold values from 0 to 4, as said below
Outputs:
- object_grad: float32 [4, 2, 4096, 768], P(None, None, ('grp', 'ty')), parts along dimension 2
The draws below stay inside these ranges and needn't reach their ends.
There are 2 independent parts, one for each index of `grp`. The reference program is written for one: setup_inputs(seed, part) draws one part's arguments, and reference() takes and returns one part's arrays. A program takes and returns all parts, laid end to end along the dimension named above; an argument that names none is the same for every part. Nothing has to cross between parts.
Inputs may be any that keep to these rules, and one draw needn't show every extreme that they name: `positions`: column 0 is a row offset under 128, column 1 a column offset of at most 640. For every device d, the counts of devices 0 to d sum to between 2 * (d + 1) and 2 * (d + 2), the upper bound reached at some device; all counts sum to 32.
All inputs are finite; a program needn't handle non-finite values.
Results may differ from the reference program's by a relative error of at most 0.0003.
Values sent between devices are 32-bit elements; how exact they have to be, the bound alone decides.
No kernel may reach another device: no remote copies, remote signals or barrier semaphores. Data moves between devices by JAX's collectives and lax.ppermute only.
A program may use at most 64 MiB of HBM per device.

```python
import jax
import jax.numpy as jnp
from jax import lax

PS = 128
NS = 4
TR = 128
OW = 768
BATCH = 2
SLOTS = 4
TILES = 16
SLOTS_ALL = 64
OROWS = 2048


def draw_counts(key, part):
    surplus = jax.random.randint(jax.random.fold_in(key, 11), (TILES,), 0, BATCH + 1)
    marker = jax.random.randint(jax.random.fold_in(key, 12), (), 0, TILES - 2)
    indices = jnp.arange(TILES)
    surplus = jnp.where(indices == marker, BATCH, surplus)
    cleared = (indices == marker - 1) | (indices == marker + 1) | (indices == TILES - 1)
    surplus = jnp.where(cleared, 0, surplus)
    before = jnp.concatenate([jnp.zeros((1,), surplus.dtype), surplus[:-1]])
    return (BATCH + surplus - before).astype(jnp.int32)


def draw_positions(key, part):
    rows_drawn = jax.random.randint(jax.random.fold_in(key, 21), (SLOTS_ALL,), 0, TR)
    cols_drawn = jax.random.randint(jax.random.fold_in(key, 22), (SLOTS_ALL,), 0, OW - PS + 1)
    chosen = jax.random.randint(jax.random.fold_in(key, 23), (), 0, SLOTS_ALL)
    indices = jnp.arange(SLOTS_ALL)
    rows_drawn = jnp.where(indices == chosen, TR - 1, rows_drawn)
    cols_drawn = jnp.where(indices == chosen, OW - PS, cols_drawn)
    return jnp.stack([rows_drawn, cols_drawn], axis=1).astype(jnp.int32)


def block_scale(key, shape, shards, smallest, top_value):
    gain = 1.0
    for axis_at, blocks in shards:
        draws = jax.random.uniform(jax.random.fold_in(jax.random.fold_in(key, 6), axis_at), (blocks,), jnp.float32, smallest / len(shards), top_value / len(shards))
        gain = gain * jnp.repeat(jnp.exp(draws), shape[axis_at] // blocks).reshape((-1,) + (1,) * (len(shape) - 1 - axis_at))
    return gain


def scatter_about(rng, extent, scale, bound, shards=(), kind=jnp.bfloat16):
    entries = jax.random.normal(rng, extent, jnp.float32) * scale
    if len(shards) > 0:
        entries = block_scale(rng, extent, shards, -0.22, 0.18) * entries
    return jnp.clip(entries, min=-bound, max=bound).astype(kind)


def setup_inputs(seed: int = 0, part: int = 0) -> dict:
    streams_of = jax.random.split(jax.random.key(seed), 7)
    part_keys = jax.random.split(jax.random.fold_in(streams_of[6], part), 7)
    tile_object = scatter_about(part_keys[0], (NS, 2, OROWS, OW), 0.7, 6.0, ((2, 16),), jnp.float32)
    probe_wave = scatter_about(streams_of[1], (2, PS, PS), 0.7, 6.0, (), jnp.float32)
    propagator_phase = jnp.clip(jax.random.uniform(streams_of[2], (PS, PS), jnp.float32, -3.140625, 3.140625), -3.140625, 3.140625)
    diffraction = jnp.clip(2.0 * jax.random.uniform(part_keys[3], (SLOTS_ALL, PS, PS), jnp.float32) ** block_scale(part_keys[3], (SLOTS_ALL, PS, PS), ((0, 16),), -0.2, 0.2), 0.0, 2.0)
    positions = draw_positions(jax.random.fold_in(jax.random.fold_in(streams_of[6], part), 71), part)
    counts = draw_counts(jax.random.fold_in(jax.random.fold_in(streams_of[6], part), 71), part)
    return {"tile_object": tile_object, "probe_wave": probe_wave, "propagator_phase": propagator_phase, "diffraction": diffraction, "positions": positions, "counts": counts}


def exit_loss(patches, probe_wave, propagator_phase, pattern):
    wavefield = lax.complex(probe_wave[0], probe_wave[1])
    kernel = lax.complex(jnp.cos(propagator_phase), jnp.sin(propagator_phase))
    for layer_index in range(NS):
        wavefield = wavefield * lax.complex(patches[layer_index, 0], patches[layer_index, 1])
        if layer_index + 1 < NS:
            spectrum = jnp.fft.fft2(wavefield, norm='ortho')
            wavefield = jnp.fft.ifft2(kernel * spectrum, norm='ortho')
    farfield = jnp.fft.fft2(wavefield, norm='ortho')
    intensity = jnp.real(farfield) ** 2 + jnp.imag(farfield) ** 2
    return jnp.sum((intensity - pattern) ** 2)

def reference(tile_object, probe_wave, propagator_phase, diffraction, positions, counts):
    padded = jnp.concatenate([tile_object, tile_object[:, :, :PS]], axis=2)
    patch_gradient = jax.grad(exit_loss)
    anchor = jnp.zeros((), jnp.int32)

    def accumulate(summed, slot_number):
        holder = slot_number // SLOTS
        is_live = (slot_number % SLOTS < counts[holder]).astype(summed.dtype)
        row_start = (holder * TR + positions[slot_number, 0]).astype(jnp.int32)
        col_start = positions[slot_number, 1].astype(jnp.int32)
        corner = (anchor, anchor, row_start, col_start)
        patches = lax.dynamic_slice(padded, corner, (NS, 2, PS, PS))
        gradient = patch_gradient(patches, probe_wave, propagator_phase, diffraction[slot_number]) * is_live
        current = lax.dynamic_slice(summed, corner, (NS, 2, PS, PS))
        return (lax.dynamic_update_slice(summed, current + gradient, corner), None)
    summed, unused = lax.scan(accumulate, jnp.zeros_like(padded), jnp.arange(SLOTS_ALL, dtype=jnp.int32))
    top_rows = summed[:, :, :PS] + summed[:, :, OROWS:]
    return jnp.concatenate([top_rows, summed[:, :, PS:OROWS]], axis=2)
```

```python
import functools

import jax
import jax.numpy as jnp
import ml_dtypes
import numpy as np
from jax import lax
from jax.experimental import pallas as pl
from jax.experimental.pallas import tpu as pltpu
from jax.sharding import PartitionSpec as P

PS = 128
PLANES = 8
SLOTS = 4
CAP = 160
F32 = jnp.float32

N_KEPT, N_MOVED = 0, 1
KEPT, MOVED = 2, 18
PLAN = 128


def shifted(x, axis, by):
    peers = lax.axis_size(axis)
    return lax.ppermute(x, axis, [(i, (i + by) % peers) for i in range(peers)])


def dft_tables():
    index = np.arange(PS)
    angle = 2.0 * np.pi * (index[:, None] * index[None, :] % PS) / PS
    re, im = np.cos(angle) / np.sqrt(PS), -np.sin(angle) / np.sqrt(PS)
    fwd = np.block([[re, im], [-im, re]])
    tables = []
    for full in (fwd, fwd.T):
        high = full.astype(ml_dtypes.bfloat16)
        tables += [high, (full - high.astype(np.float64)).astype(ml_dtypes.bfloat16)]
    return np.stack(tables)


def plan_kernel(pos_ref, count_ref, plan_ref):
    count = count_ref[0]
    rows = [pos_ref[j, 0] for j in range(SLOTS)]
    best_score, best_set = jnp.int32(1 << 30), jnp.int32(0)
    for chosen in range(1 << SLOTS):
        up = down = kept = moved = jnp.int32(0)
        for j in range(SLOTS):
            live = (count > j).astype(jnp.int32)
            if chosen >> j & 1:
                down, moved = down + live * (PS - rows[j]), moved + live
            else:
                up, kept = up + live * rows[j], kept + live
        most = jnp.maximum(up, down)
        score = (
            most
            + jnp.where(most > CAP, 1 << 20, 0)
            + jnp.where(kept > 2, 1 << 10, 0)
            + jnp.where(moved > 2, 1 << 10, 0)
        )
        better = score < best_score
        best_score = jnp.where(better, score, best_score)
        best_set = jnp.where(better, chosen, best_set)
    for j in range(SLOTS):
        for base in (KEPT, MOVED):
            for field in range(4):
                plan_ref[base + 4 * field + j] = 0
    n = [jnp.int32(0), jnp.int32(0)]
    offset = [jnp.int32(0), jnp.int32(0)]
    spare = PLAN - 16
    for j in range(SLOTS):
        live = count > j
        moved = (best_set >> j) & 1
        for side, base in ((0, KEPT), (1, MOVED)):
            mine = jnp.logical_and(live, moved == side)
            at = jnp.where(mine, base + n[side], spare)
            plan_ref[at] = rows[j]
            plan_ref[at + 4] = pos_ref[j, 1]
            plan_ref[at + 8] = offset[side]
            plan_ref[at + 12] = j
            taken = PS - rows[j] if side else rows[j]
            n[side] = n[side] + mine.astype(jnp.int32)
            offset[side] = offset[side] + jnp.where(mine, taken, 0)
    plan_ref[N_KEPT] = n[0]
    plan_ref[N_MOVED] = n[1]


def make_plan(positions, counts):
    return pl.pallas_call(
        plan_kernel,
        out_shape=jax.ShapeDtypeStruct((PLAN,), jnp.int32),
        in_specs=[pl.BlockSpec(memory_space=pltpu.SMEM)] * 2,
        out_specs=pl.BlockSpec(memory_space=pltpu.SMEM),
        name="plan",
    )(positions, counts)


def lanes():
    return lax.broadcasted_iota(jnp.int32, (PS, PS), 1)


def column_blocks(col, blocks):
    first = col // PS
    return first, jnp.minimum(first + 1, blocks - 1), col % PS


def blocked(planes, rows, width):
    return pltpu.VMEM((planes, width // PS, rows, PS), F32)


def fill(buf, at, ref):
    for block in range(buf.shape[1]):
        buf[:, block, pl.ds(at, ref.shape[1]), :] = ref[:, :, block * PS : (block + 1) * PS]


def empty(buf, at, ref):
    for block in range(buf.shape[1]):
        ref[:, :, block * PS : (block + 1) * PS] = buf[:, block, pl.ds(at, ref.shape[1]), :]


def read_window(buf, plane, row, col):
    first, second, part = column_blocks(col, buf.shape[1])
    back = (PS - part) & (PS - 1)
    left = pltpu.roll(buf[plane, first, pl.ds(row, PS), :], back, 1)
    right = pltpu.roll(buf[plane, second, pl.ds(row, PS), :], back, 1)
    return jnp.where(lanes() < PS - part, left, right)


def add_window(buf, plane, row, col, value):
    first, second, part = column_blocks(col, buf.shape[1])
    value = pltpu.roll(value, part, 1)
    here = lanes() >= part
    buf[plane, first, pl.ds(row, PS), :] += jnp.where(here, value, 0.0)
    buf[plane, second, pl.ds(row, PS), :] += jnp.where(here, 0.0, value)


def pack_kernel(moved, plan_ref, tile_ref, out_ref, tile, packed):
    planes = tile_ref.shape[0]
    fill(tile, 0, tile_ref)
    base = MOVED if moved else KEPT

    @pl.loop(0, plan_ref[N_MOVED if moved else N_KEPT])
    def _(k):
        row, col, offset = plan_ref[base + k], plan_ref[base + 4 + k], plan_ref[base + 8 + k]
        start = row if moved else 0
        for plane in range(planes):
            packed[plane, pl.ds(offset, PS), :] = read_window(tile, plane, start, col)

    out_ref[...] = packed[:, :CAP, :]


def pack(moved, plan, tile, step):
    planes, rows, width = tile.shape
    return pl.pallas_call(
        functools.partial(pack_kernel, moved),
        grid=(planes // step,),
        out_shape=jax.ShapeDtypeStruct((planes, CAP, PS), F32),
        in_specs=[
            pl.BlockSpec(memory_space=pltpu.SMEM),
            pl.BlockSpec((step, rows, width), lambda i: (i, 0, 0)),
        ],
        out_specs=pl.BlockSpec((step, CAP, PS), lambda i: (i, 0, 0)),
        scratch_shapes=[
            blocked(step, rows + PS, width),
            pltpu.VMEM((step, CAP + PS, PS), F32),
        ],
        compiler_params=pltpu.CompilerParams(vmem_limit_bytes=32 * 1024 * 1024),
        cost_estimate=pl.CostEstimate(flops=0, bytes_accessed=8 * 1024 * 1024, transcendentals=0),
        name="pack_moved" if moved else "pack_kept",
    )(plan, tile)


def split(x):
    high = x.astype(jnp.bfloat16)
    return high, (x - high.astype(F32)).astype(jnp.bfloat16)


def dot(a, b):
    return jnp.dot(a, b, preferred_element_type=F32)


def times_table(x, table):
    high, low = split(x)
    return dot(low, table[0]) + dot(high, table[1]) + dot(high, table[0])


def table_times(table, x):
    high, low = split(x)
    return dot(table[0], low) + dot(table[1], high) + dot(table[0], high)


def swap(x):
    return jnp.concatenate(
        [
            jnp.concatenate([x[:PS, :PS], x[PS:, :PS]], axis=1),
            jnp.concatenate([x[:PS, PS:], x[PS:, PS:]], axis=1),
        ],
        axis=0,
    )


def wave_kernel(
    moved, plan_ref, tile_ref, msg_ref, pattern_ref, probe_ref, prop_ref, table_ref,
    grads_ref, out_ref, tile, msg, patch, grad, waves, packed,
):
    fill(tile, 0, tile_ref)
    msg[:, :CAP, :] = msg_ref[...]
    base = MOVED if moved else KEPT
    count = plan_ref[N_MOVED if moved else N_KEPT]
    layers = PLANES // 2
    fwd = (table_ref[0], table_ref[1])
    bwd = (table_ref[2], table_ref[3])
    prop_re = jnp.concatenate([prop_ref[0]] * 2, axis=1)
    prop_im = jnp.concatenate([prop_ref[1]] * 2, axis=1)

    def dft(x):
        return table_times(bwd, swap(times_table(x, fwd)))

    def inverse(x):
        return times_table(swap(table_times(fwd, x)), bwd)

    def cols(x):
        return x[:, :PS], x[:, PS:]

    @pl.loop(0, (count + 1) // 2)
    def _(pair):
        ks = [2 * pair, jnp.minimum(2 * pair + 1, count - 1)]
        for i, k in enumerate(ks):
            row, col, offset = plan_ref[base + k], plan_ref[base + 4 + k], plan_ref[base + 8 + k]
            for plane in range(PLANES):
                if moved:
                    patch[i, plane, :PS, :] = msg[plane, pl.ds(offset, PS), :]
                    patch[i, plane, pl.ds(PS - row, PS), :] = read_window(tile, plane, 0, col)
                else:
                    patch[i, plane, :PS, :] = read_window(tile, plane, row, col)
                    patch[i, plane, pl.ds(PS - row, PS), :] = msg[plane, pl.ds(offset, PS), :]

        def parts(layer):
            re = jnp.concatenate([patch[i, 2 * layer, :PS, :] for i in range(2)], axis=0)
            im = jnp.concatenate([patch[i, 2 * layer + 1, :PS, :] for i in range(2)], axis=0)
            return re, im

        def propagate(x, sign):
            y = dft(x)
            re, im = y[:PS], y[PS:]
            k_im = prop_im * sign
            y = jnp.concatenate([re * prop_re - im * k_im, re * k_im + im * prop_re], axis=0)
            return inverse(y)

        probe = jnp.concatenate([probe_ref[0], probe_ref[1]], axis=1)
        waves[0] = jnp.concatenate([probe, probe], axis=0)
        for layer in range(layers):
            t_re, t_im = parts(layer)
            re, im = cols(waves[layer])
            x = jnp.concatenate([re * t_re - im * t_im, re * t_im + im * t_re], axis=1)
            if layer + 1 < layers:
                waves[layer + 1] = propagate(x, 1.0)
        far = dft(x)
        re, im = far[:PS], far[PS:]
        pattern = jnp.concatenate(
            [pattern_ref[plan_ref[base + 12 + k]] for k in ks], axis=1
        )
        scale = 4.0 * (re * re + im * im - pattern)
        x = inverse(jnp.concatenate([scale * re, scale * im], axis=0))
        for layer in reversed(range(layers)):
            g_re, g_im = cols(x)
            w_re, w_im = cols(waves[layer])
            d_re = w_re * g_re + w_im * g_im
            d_im = w_re * g_im - w_im * g_re
            for i in range(2):
                grad[i, 2 * layer, :PS, :] = d_re[i * PS : (i + 1) * PS]
                grad[i, 2 * layer + 1, :PS, :] = d_im[i * PS : (i + 1) * PS]
            if layer:
                t_re, t_im = parts(layer)
                x = jnp.concatenate(
                    [t_re * g_re + t_im * g_im, t_re * g_im - t_im * g_re], axis=1
                )
                x = propagate(x, -1.0)

        for i, k in enumerate(ks):
            row, offset = plan_ref[base + k], plan_ref[base + 8 + k]
            grads_ref[k] = grad[i, :, :PS, :]
            for plane in range(PLANES):
                if moved:
                    far_rows = grad[i, plane, :PS, :]
                else:
                    far_rows = grad[i, plane, pl.ds(PS - row, PS), :]
                packed[plane, pl.ds(offset, PS), :] = far_rows

    out_ref[...] = packed[:, :CAP, :]


def gradients(moved, plan, tile, msg, patterns, probe, prop, tables):
    planes, rows, width = tile.shape
    vmem = pl.BlockSpec(memory_space=pltpu.VMEM)
    return pl.pallas_call(
        functools.partial(wave_kernel, moved),
        out_shape=(
            jax.ShapeDtypeStruct((SLOTS, planes, PS, PS), F32),
            jax.ShapeDtypeStruct((planes, CAP, PS), F32),
        ),
        in_specs=[pl.BlockSpec(memory_space=pltpu.SMEM)] + [vmem] * 6,
        out_specs=(vmem, vmem),
        scratch_shapes=[
            blocked(planes, rows + PS, width),
            pltpu.VMEM((planes, CAP + PS, PS), F32),
            pltpu.VMEM((2, planes, 2 * PS, PS), F32),
            pltpu.VMEM((2, planes, 2 * PS, PS), F32),
            pltpu.VMEM((planes // 2, 2 * PS, 2 * PS), F32),
            pltpu.VMEM((planes, CAP + PS, PS), F32),
        ],
        compiler_params=pltpu.CompilerParams(vmem_limit_bytes=48 * 1024 * 1024),
        cost_estimate=pl.CostEstimate(
            flops=6 * 1024**3, bytes_accessed=8 * 1024 * 1024, transcendentals=0
        ),
        name="waves_moved" if moved else "waves_kept",
    )(plan, tile, msg, patterns, probe, prop, tables)


def deposit_kernel(plan_ref, above_ref, kept_ref, moved_ref, out_ref, acc):
    acc[...] = jnp.zeros_like(acc)

    @pl.loop(0, plan_ref[N_KEPT])
    def _(k):
        row, col = plan_ref[KEPT + k], plan_ref[KEPT + 4 + k]
        for plane in range(out_ref.shape[0]):
            add_window(acc, plane, PS + row, col, kept_ref[k, plane])

    @pl.loop(0, above_ref[N_MOVED])
    def _(k):
        row, col = above_ref[MOVED + k], above_ref[MOVED + 4 + k]
        for plane in range(out_ref.shape[0]):
            add_window(acc, plane, row, col, moved_ref[k, plane])

    empty(acc, PS, out_ref)


def deposit(plan, above, kept, moved, shape, step):
    planes, rows, width = shape
    smem = pl.BlockSpec(memory_space=pltpu.SMEM)
    part = pl.BlockSpec((SLOTS, step, PS, PS), lambda i: (0, i, 0, 0))
    return pl.pallas_call(
        deposit_kernel,
        grid=(planes // step,),
        out_shape=jax.ShapeDtypeStruct(shape, F32),
        in_specs=[smem, smem, part, part],
        out_specs=pl.BlockSpec((step, rows, width), lambda i: (i, 0, 0)),
        scratch_shapes=[blocked(step, rows + 2 * PS, width)],
        compiler_params=pltpu.CompilerParams(vmem_limit_bytes=32 * 1024 * 1024),
        cost_estimate=pl.CostEstimate(flops=0, bytes_accessed=8 * 1024 * 1024, transcendentals=0),
        name="deposit",
    )(plan, above, kept, moved)


def finish_kernel(plan_ref, above_ref, sum_ref, up_ref, down_ref, out_ref, acc, msg):
    planes = out_ref.shape[0]
    fill(acc, 0, sum_ref)
    msg[:, :CAP, :] = up_ref[...]

    @pl.loop(0, plan_ref[N_MOVED])
    def _(k):
        row, col, offset = (plan_ref[MOVED + 4 * i + k] for i in range(3))
        for plane in range(planes):
            add_window(acc, plane, row, col, msg[plane, pl.ds(offset, PS), :])

    msg[:, :CAP, :] = down_ref[...]

    @pl.loop(0, above_ref[N_KEPT])
    def _(k):
        row, col, offset = (above_ref[KEPT + 4 * i + k] for i in range(3))
        inside = lax.broadcasted_iota(jnp.int32, (PS, PS), 0) < row
        for plane in range(planes):
            value = jnp.where(inside, msg[plane, pl.ds(offset, PS), :], 0.0)
            add_window(acc, plane, 0, col, value)

    empty(acc, 0, out_ref)


def finish(plan, above, summed, from_below, from_above, step):
    planes, rows, width = summed.shape
    smem = pl.BlockSpec(memory_space=pltpu.SMEM)
    whole = pl.BlockSpec((step, rows, width), lambda i: (i, 0, 0))
    part = pl.BlockSpec((step, CAP, PS), lambda i: (i, 0, 0))
    return pl.pallas_call(
        finish_kernel,
        grid=(planes // step,),
        out_shape=jax.ShapeDtypeStruct(summed.shape, F32),
        in_specs=[smem, smem, whole, part, part],
        out_specs=whole,
        scratch_shapes=[
            blocked(step, rows + PS, width),
            pltpu.VMEM((step, CAP + PS, PS), F32),
        ],
        compiler_params=pltpu.CompilerParams(vmem_limit_bytes=32 * 1024 * 1024),
        cost_estimate=pl.CostEstimate(flops=0, bytes_accessed=8 * 1024 * 1024, transcendentals=0),
        name="finish",
    )(plan, above, summed, from_below, from_above)


def per_device(tile_object, probe_wave, propagator_phase, diffraction, positions, counts):
    layers, two, rows, width = tile_object.shape
    tile = tile_object.reshape(layers * two, rows, width)
    patterns_above = shifted(diffraction, "ty", 1)
    plan = make_plan(positions, counts)
    above = shifted(plan, "ty", 1)
    prop = jnp.stack([jnp.cos(propagator_phase), jnp.sin(propagator_phase)])
    tables = jnp.asarray(dft_tables())

    rows_above = shifted(pack(True, plan, tile, 2), "ty", 1)
    rows_below = shifted(pack(False, above, tile, 2), "ty", -1)
    moved, back_up = gradients(True, above, tile, rows_above, patterns_above, probe_wave, prop, tables)
    from_below = shifted(back_up, "ty", -1)
    kept, back_down = gradients(False, plan, tile, rows_below, diffraction, probe_wave, prop, tables)
    from_above = shifted(back_down, "ty", 1)
    summed = deposit(plan, above, kept, moved, tile.shape, 2)
    out = finish(plan, above, summed, from_below, from_above, 2)
    return out.reshape(tile_object.shape)


def solution(mesh):
    in_specs = (
        P(None, None, ("grp", "ty"), None),
        P(),
        P(),
        P(("grp", "ty"), None, None),
        P(("grp", "ty"), None),
        P(("grp", "ty")),
    )
    out_specs = P(None, None, ("grp", "ty"), None)
    return jax.shard_map(
        per_device, mesh=mesh, in_specs=in_specs, out_specs=out_specs, check_vma=False
    )
```

```python
import functools

import jax
import jax.numpy as jnp
import ml_dtypes
import numpy as np
from jax import lax
from jax.experimental import pallas as pl
from jax.experimental.pallas import tpu as pltpu
from jax.sharding import PartitionSpec as P

PS = 128
PLANES = 8
SLOTS = 4
CAP = 160
F32 = jnp.float32

N_KEPT, N_MOVED = 0, 1
KEPT, MOVED = 2, 18
PLAN = 128

CHAINS = 4
PACK_VMEM = 8 * 1024 * 1024
WAVE_VMEM = 20 * 1024 * 1024


def shifted(x, axis, by):
    peers = lax.axis_size(axis)
    return lax.ppermute(x, axis, [(i, (i + by) % peers) for i in range(peers)])


def dft_tables():
    index = np.arange(PS)
    angle = 2.0 * np.pi * (index[:, None] * index[None, :] % PS) / PS
    re, im = np.cos(angle) / np.sqrt(PS), -np.sin(angle) / np.sqrt(PS)
    fwd = np.block([[re, im], [-im, re]])
    tables = []
    for full in (fwd, fwd.T):
        high = full.astype(ml_dtypes.bfloat16)
        tables += [high, (full - high.astype(np.float64)).astype(ml_dtypes.bfloat16)]
    return np.stack(tables)


def write_plan(pos_ref, count_ref, plan_ref):
    count = count_ref[0]
    rows = [pos_ref[0, j] for j in range(SLOTS)]
    best_score, best_set = jnp.int32(1 << 30), jnp.int32(0)
    for chosen in range(1 << SLOTS):
        up = down = kept = moved = jnp.int32(0)
        for j in range(SLOTS):
            live = (count > j).astype(jnp.int32)
            if chosen >> j & 1:
                down, moved = down + live * (PS - rows[j]), moved + live
            else:
                up, kept = up + live * rows[j], kept + live
        most = jnp.maximum(up, down)
        score = (
            most
            + jnp.where(most > CAP, 1 << 20, 0)
            + jnp.where(kept > 2, 1 << 10, 0)
            + jnp.where(moved > 2, 1 << 10, 0)
        )
        better = score < best_score
        best_score = jnp.where(better, score, best_score)
        best_set = jnp.where(better, chosen, best_set)
    for j in range(SLOTS):
        for base in (KEPT, MOVED):
            for field in range(4):
                plan_ref[base + 4 * field + j] = 0
    n = [jnp.int32(0), jnp.int32(0)]
    offset = [jnp.int32(0), jnp.int32(0)]
    spare = PLAN - 16
    for j in range(SLOTS):
        live = count > j
        moved = (best_set >> j) & 1
        for side, base in ((0, KEPT), (1, MOVED)):
            mine = jnp.logical_and(live, moved == side)
            at = jnp.where(mine, base + n[side], spare)
            plan_ref[at] = rows[j]
            plan_ref[at + 4] = pos_ref[1, j]
            plan_ref[at + 8] = offset[side]
            plan_ref[at + 12] = j
            taken = PS - rows[j] if side else rows[j]
            n[side] = n[side] + mine.astype(jnp.int32)
            offset[side] = offset[side] + jnp.where(mine, taken, 0)
    plan_ref[N_KEPT] = n[0]
    plan_ref[N_MOVED] = n[1]


def lanes():
    return lax.broadcasted_iota(jnp.int32, (PS, PS), 1)


def sublanes():
    return lax.broadcasted_iota(jnp.int32, (PS, PS), 0)


def column_blocks(col, width):
    first = pl.multiple_of((col // PS) * PS, PS)
    second = pl.multiple_of(jnp.minimum(first + PS, width - PS), PS)
    return first, second, col % PS


def shifted_columns(left, right, by):
    back = (PS - by) & (PS - 1)
    return jnp.where(lanes() < PS - by, pltpu.roll(left, back, 1), pltpu.roll(right, back, 1))


def read_columns(ref, plane, col):
    first, second, part = column_blocks(col, ref.shape[-1])
    return shifted_columns(ref[plane, :, pl.ds(first, PS)], ref[plane, :, pl.ds(second, PS)], part)


def add_columns(ref, plane, col, value):
    first, second, part = column_blocks(col, ref.shape[-1])
    value = pltpu.roll(value, part, 1)
    here = lanes() >= part
    ref[plane, :, pl.ds(first, PS)] += jnp.where(here, value, 0.0)
    ref[plane, :, pl.ds(second, PS)] += jnp.where(here, 0.0, value)


def entry(plan_ref, base, k):
    return plan_ref[base + k], plan_ref[base + 4 + k], plan_ref[base + 8 + k]


def pack_moved_kernel(pos_ref, count_ref, tile_ref, packed_ref, plan, columns, packed, sems):
    write_plan(pos_ref, count_ref, plan)
    count = plan[N_MOVED]

    def fetch(k):
        start = pl.multiple_of(plan[MOVED + 4 + k] // PS * PS, PS)
        start = pl.multiple_of(jnp.minimum(start, tile_ref.shape[2] - 2 * PS), PS)
        source = tile_ref.at[:, :, pl.ds(start, 2 * PS)]
        return pltpu.make_async_copy(source, columns.at[k], sems.at[k]), start

    for k in range(SLOTS):

        @pl.when(k < count)
        def _(k=k):
            fetch(k)[0].start()

    for k in reversed(range(SLOTS)):

        @pl.when(k < count)
        def _(k=k):
            row, col, offset = entry(plan, MOVED, k)
            copy, start = fetch(k)
            copy.wait()
            for plane in range(PLANES):
                value = shifted_columns(
                    columns[k, plane, :, :PS], columns[k, plane, :, PS:], col - start
                )
                packed[plane, pl.ds(PS + offset - row, PS), :] = value

    packed_ref[...] = packed[:, PS : PS + CAP, :]


def pack_moved(positions, counts, tile):
    planes, rows, _ = tile.shape
    smem = pl.BlockSpec(memory_space=pltpu.SMEM)
    return pl.pallas_call(
        pack_moved_kernel,
        out_shape=jax.ShapeDtypeStruct((planes, CAP, PS), F32),
        in_specs=[smem, smem, pl.BlockSpec(memory_space=pl.ANY)],
        out_specs=pl.BlockSpec(memory_space=pltpu.VMEM),
        scratch_shapes=[
            pltpu.SMEM((PLAN,), jnp.int32),
            pltpu.VMEM((SLOTS, planes, rows, 2 * PS), F32),
            pltpu.VMEM((planes, CAP + 2 * PS, PS), F32),
            pltpu.SemaphoreType.DMA((SLOTS,)),
        ],
        compiler_params=pltpu.CompilerParams(vmem_limit_bytes=PACK_VMEM),
        cost_estimate=pl.CostEstimate(flops=0, bytes_accessed=4 * 1024 * 1024, transcendentals=0),
        name="pack_moved",
    )(positions, counts, tile)


def parts_kernel(
    pos_ref, count_ref, pos_above_ref, count_above_ref, tile_ref,
    packed_ref, kept_ref, moved_ref, plan, above, packed,
):
    write_plan(pos_above_ref, count_above_ref, above)

    @pl.loop(0, above[N_KEPT])
    def _(k):
        _, col, offset = entry(above, KEPT, k)
        for plane in range(PLANES):
            packed[plane, pl.ds(offset, PS), :] = read_columns(tile_ref, plane, col)

    packed_ref[...] = packed[:, :CAP, :]
    write_plan(pos_ref, count_ref, plan)

    @pl.loop(0, plan[N_KEPT])
    def _(k):
        for plane in range(PLANES):
            kept_ref[k, plane] = read_columns(tile_ref, plane, plan[KEPT + 4 + k])

    @pl.loop(0, above[N_MOVED])
    def _(k):
        for plane in range(PLANES):
            moved_ref[k, plane] = read_columns(tile_ref, plane, above[MOVED + 4 + k])


def parts(where, tile):
    planes = tile.shape[0]
    smem = pl.BlockSpec(memory_space=pltpu.SMEM)
    vmem = pl.BlockSpec(memory_space=pltpu.VMEM)
    windows = jax.ShapeDtypeStruct((SLOTS, planes, PS, PS), F32)
    return pl.pallas_call(
        parts_kernel,
        out_shape=(jax.ShapeDtypeStruct((planes, CAP, PS), F32), windows, windows),
        in_specs=[smem] * 4 + [vmem],
        out_specs=(vmem, vmem, vmem),
        scratch_shapes=[
            pltpu.SMEM((PLAN,), jnp.int32),
            pltpu.SMEM((PLAN,), jnp.int32),
            pltpu.VMEM((planes, CAP + PS, PS), F32),
        ],
        compiler_params=pltpu.CompilerParams(vmem_limit_bytes=PACK_VMEM),
        cost_estimate=pl.CostEstimate(flops=0, bytes_accessed=8 * 1024 * 1024, transcendentals=0),
        name="parts",
    )(*where, tile)


def split(x):
    high = x.astype(jnp.bfloat16)
    return high, (x - high.astype(F32)).astype(jnp.bfloat16)


def dot(a, b):
    return jnp.dot(a, b, preferred_element_type=F32)


def times_table(x, table):
    high, low = split(x)
    return dot(low, table[0]) + dot(high, table[1]) + dot(high, table[0])


def turned(x):
    return jnp.concatenate([x[:, :PS].T, x[:, PS:].T], axis=1)


def halves(x):
    return x[:, :PS], x[:, PS:]


def times(a, b):
    (a_re, a_im), (b_re, b_im) = a, b
    return jnp.concatenate([a_re * b_re - a_im * b_im, a_re * b_im + a_im * b_re], axis=1)


def times_conj(a, b):
    (a_re, a_im), (b_re, b_im) = a, b
    return jnp.concatenate([a_re * b_re + a_im * b_im, a_im * b_re - a_re * b_im], axis=1)


def wave_kernel(
    moved, pos_ref, count_ref, own_ref, msg_ref, pattern_ref, probe_ref, prop_ref, table_ref,
    *refs,
):
    grads_ref, out_ref, plan_ref, msg, patch, grad, waves, packed = refs[-8:]
    write_plan(pos_ref, count_ref, plan_ref)
    msg[:, :CAP, :] = msg_ref[...]
    base = MOVED if moved else KEPT
    count = plan_ref[N_MOVED if moved else N_KEPT]
    layers = PLANES // 2
    chains = range(patch.shape[0])
    fwd = (table_ref[0], table_ref[1])
    bwd = (table_ref[2], table_ref[3])

    def transform(xs, table):
        return [times_table(turned(times_table(x, table)), table) for x in xs]

    def propagate(xs, product):
        prop = (prop_ref[0], prop_ref[1])
        xs = [product(halves(x), prop) for x in transform(xs, fwd)]
        return transform(xs, bwd)

    def layer_of(i, layer):
        return patch[i, 2 * layer, PS : 2 * PS, :], patch[i, 2 * layer + 1, PS : 2 * PS, :]

    @pl.loop(0, (count + len(chains) - 1) // len(chains))
    def _(group):
        first = group * len(chains)
        for i in chains:

            @pl.when(first + i < count)
            def _(i=i, k=first + i):
                row, _, offset = entry(plan_ref, base, k)
                for plane in range(PLANES):
                    own, other = own_ref[k, plane], msg[plane, pl.ds(offset, PS), :]
                    if moved:
                        patch[i, plane, PS : 2 * PS, :] = other
                        patch[i, plane, pl.ds(2 * PS - row, PS), :] = own
                    else:
                        patch[i, plane, pl.ds(PS - row, PS), :] = own
                        patch[i, plane, pl.ds(2 * PS - row, PS), :] = other

        probe = (probe_ref[0], probe_ref[1])
        for layer in range(layers):
            xs = []
            for i in chains:
                wave = halves(waves[layer, i]) if layer else probe
                xs.append(times(wave, layer_of(i, layer)))
            if layer + 1 < layers:
                for i, x in enumerate(propagate(xs, times)):
                    waves[layer + 1, i] = x
        xs = transform(xs, fwd)
        for i in chains:
            slot = plan_ref[base + 12 + jnp.minimum(first + i, SLOTS - 1)]
            re, im = halves(xs[i])
            scale = 4.0 * (re * re + im * im - pattern_ref[slot].T)
            xs[i] = jnp.concatenate([scale * re, scale * im], axis=1)
        xs = transform(xs, bwd)
        for layer in reversed(range(layers)):
            for i in chains:
                wave = halves(waves[layer, i]) if layer else probe
                d_re, d_im = halves(times_conj(halves(xs[i]), wave))
                grad[i, 2 * layer, :PS, :] = d_re
                grad[i, 2 * layer + 1, :PS, :] = d_im
                if layer:
                    xs[i] = times_conj(halves(xs[i]), layer_of(i, layer))
            if layer:
                xs = propagate(xs, times_conj)

        for i in chains:

            @pl.when(first + i < count)
            def _(i=i, k=first + i):
                row, _, offset = entry(plan_ref, base, k)
                grads_ref[k] = grad[i, :, :PS, :]
                for plane in range(PLANES):
                    start = 0 if moved else PS - row
                    packed[plane, pl.ds(offset, PS), :] = grad[i, plane, pl.ds(start, PS), :]

    out_ref[...] = packed[:, :CAP, :]


def gradients(moved, positions, counts, own, msg, patterns, probe, prop, tables, after=()):
    planes = own.shape[1]
    smem = pl.BlockSpec(memory_space=pltpu.SMEM)
    vmem = pl.BlockSpec(memory_space=pltpu.VMEM)
    return pl.pallas_call(
        functools.partial(wave_kernel, moved),
        out_shape=(
            jax.ShapeDtypeStruct((SLOTS, planes, PS, PS), F32),
            jax.ShapeDtypeStruct((planes, CAP, PS), F32),
        ),
        in_specs=[smem] * 2 + [vmem] * 6 + [pl.BlockSpec(memory_space=pl.ANY)] * len(after),
        out_specs=(vmem, vmem),
        scratch_shapes=[
            pltpu.SMEM((PLAN,), jnp.int32),
            pltpu.VMEM((planes, CAP + PS, PS), F32),
            pltpu.VMEM((CHAINS, planes, 3 * PS, PS), F32),
            pltpu.VMEM((CHAINS, planes, 2 * PS, PS), F32),
            pltpu.VMEM((planes // 2, CHAINS, PS, 2 * PS), F32),
            pltpu.VMEM((planes, CAP + PS, PS), F32),
        ],
        compiler_params=pltpu.CompilerParams(vmem_limit_bytes=WAVE_VMEM),
        cost_estimate=pl.CostEstimate(
            flops=6 * 1024**3, bytes_accessed=8 * 1024 * 1024, transcendentals=0
        ),
        name="waves_moved" if moved else "waves_kept",
    )(positions, counts, own, msg, patterns, probe, prop, tables, *after)


def deposit_kernel(
    pos_ref, count_ref, pos_above_ref, count_above_ref, kept_ref, moved_ref, below_ref, out_ref, plan, above, shift
):
    write_plan(pos_ref, count_ref, plan)
    write_plan(pos_above_ref, count_above_ref, above)
    out_ref[...] = jnp.zeros_like(out_ref)

    @pl.loop(0, plan[N_KEPT])
    def _(k):
        row, col, _ = entry(plan, KEPT, k)
        inside = sublanes() >= row
        for plane in range(PLANES):
            shift[plane, pl.ds(row, PS), :] = kept_ref[k, plane]
            add_columns(out_ref, plane, col, jnp.where(inside, shift[plane, :PS, :], 0.0))

    @pl.loop(0, above[N_MOVED])
    def _(k):
        row, col, _ = entry(above, MOVED, k)
        inside = sublanes() < row
        for plane in range(PLANES):
            shift[plane, pl.ds(row, PS), :] = moved_ref[k, plane]
            add_columns(out_ref, plane, col, jnp.where(inside, shift[plane, PS : 2 * PS, :], 0.0))

    shift[:, PS : PS + CAP, :] = below_ref[...]

    @pl.loop(0, plan[N_MOVED])
    def _(k):
        row, col, offset = entry(plan, MOVED, k)
        inside = sublanes() >= row
        for plane in range(PLANES):
            value = shift[plane, pl.ds(PS + offset - row, PS), :]
            add_columns(out_ref, plane, col, jnp.where(inside, value, 0.0))


def deposit(where, kept, moved, from_below, shape):
    planes = shape[0]
    smem = pl.BlockSpec(memory_space=pltpu.SMEM)
    vmem = pl.BlockSpec(memory_space=pltpu.VMEM)
    return pl.pallas_call(
        deposit_kernel,
        out_shape=jax.ShapeDtypeStruct(shape, F32),
        in_specs=[smem] * 4 + [vmem] * 3,
        out_specs=vmem,
        scratch_shapes=[pltpu.SMEM((PLAN,), jnp.int32)] * 2
        + [pltpu.VMEM((planes, CAP + 2 * PS, PS), F32)],
        compiler_params=pltpu.CompilerParams(vmem_limit_bytes=PACK_VMEM),
        cost_estimate=pl.CostEstimate(flops=0, bytes_accessed=4 * 1024 * 1024, transcendentals=0),
        name="deposit",
    )(*where, kept, moved, from_below)


def finish_kernel(pos_ref, count_ref, sum_ref, msg_ref, out_ref, plan, total, msg, sems):
    write_plan(pos_ref, count_ref, plan)
    msg[:, :CAP, :] = msg_ref[...]
    copies = []
    for plane in range(PLANES):
        total[plane] = sum_ref[plane]

        @pl.loop(0, plan[N_KEPT])
        def _(k, plane=plane):
            row, col, offset = entry(plan, KEPT, k)
            value = jnp.where(sublanes() < row, msg[plane, pl.ds(offset, PS), :], 0.0)
            add_columns(total, plane, col, value)

        copy = pltpu.make_async_copy(total.at[plane], out_ref.at[plane], sems.at[plane])
        copy.start()
        copies.append(copy)
    for copy in copies:
        copy.wait()


def finish(positions_above, counts_above, summed, from_above):
    planes = summed.shape[0]
    smem = pl.BlockSpec(memory_space=pltpu.SMEM)
    vmem = pl.BlockSpec(memory_space=pltpu.VMEM)
    return pl.pallas_call(
        finish_kernel,
        out_shape=jax.ShapeDtypeStruct(summed.shape, F32),
        in_specs=[smem, smem, vmem, vmem],
        out_specs=pl.BlockSpec(memory_space=pl.ANY),
        scratch_shapes=[
            pltpu.SMEM((PLAN,), jnp.int32),
            pltpu.VMEM(summed.shape, F32),
            pltpu.VMEM((planes, CAP + PS, PS), F32),
            pltpu.SemaphoreType.DMA((planes,)),
        ],
        compiler_params=pltpu.CompilerParams(vmem_limit_bytes=PACK_VMEM),
        cost_estimate=pl.CostEstimate(flops=0, bytes_accessed=4 * 1024 * 1024, transcendentals=0),
        name="finish",
    )(positions_above, counts_above, summed, from_above)


def per_device(tile_object, probe_wave, propagator_phase, diffraction, positions, counts):
    layers, two, rows, width = tile_object.shape
    tile = tile_object.reshape(layers * two, rows, width)
    positions = positions.T
    positions_above = shifted(positions, "ty", 1)
    counts_above = shifted(counts, "ty", 1)
    patterns_above = shifted(diffraction, "ty", 1)
    phase = propagator_phase.T
    prop = jnp.stack([jnp.cos(phase), jnp.sin(phase)])
    tables = jnp.asarray(dft_tables())

    down = pack_moved(positions, counts, tile)
    down, positions_above, counts_above, patterns_above = lax.optimization_barrier(
        (down, positions_above, counts_above, patterns_above)
    )
    rows_above = shifted(down, "ty", 1)
    where = (positions, counts, positions_above, counts_above)
    up, own_kept, own_moved = parts(where, tile)
    up, rows_above = lax.optimization_barrier((up, rows_above))
    rows_below = shifted(up, "ty", -1)
    moved, back_up = gradients(
        True, positions_above, counts_above, own_moved, rows_above, patterns_above,
        probe_wave, prop, tables,
    )
    from_below = shifted(back_up, "ty", -1)
    kept, back_down = gradients(
        False, positions, counts, own_kept, rows_below, diffraction,
        probe_wave, prop, tables, after=(moved,),
    )
    from_above = shifted(back_down, "ty", 1)
    summed = deposit(where, kept, moved, from_below, tile.shape)
    out = finish(positions_above, counts_above, summed, from_above)
    return out.reshape(tile_object.shape)


def solution(mesh):
    in_specs = (
        P(None, None, ("grp", "ty"), None),
        P(),
        P(),
        P(("grp", "ty"), None, None),
        P(("grp", "ty"), None),
        P(("grp", "ty")),
    )
    out_specs = P(None, None, ("grp", "ty"), None)
    return jax.shard_map(
        per_device, mesh=mesh, in_specs=in_specs, out_specs=out_specs, check_vma=False
    )
```

```python
import functools

import jax
import jax.numpy as jnp
import ml_dtypes
import numpy as np
from jax import lax
from jax.experimental import pallas as pl
from jax.experimental.pallas import tpu as pltpu
from jax.sharding import PartitionSpec as P

PS = 128
PLANES = 8
SLOTS = 4
CAP_KEPT, CAP_MOVED = 152, 160
F32 = jnp.float32

N_KEPT, N_MOVED = 0, 1
KEPT, MOVED = 2, 18
PLAN = 128

CHAINS = 4
PACK_VMEM = 8 * 1024 * 1024
PACK_MOVED_VMEM = 60 * 1024 * 1024
WAVE_VMEM = 20 * 1024 * 1024


def shifted(x, axis, by):
    peers = lax.axis_size(axis)
    return lax.ppermute(x, axis, [(i, (i + by) % peers) for i in range(peers)])


def dft_tables():
    index = np.arange(PS)
    angle = 2.0 * np.pi * (index[:, None] * index[None, :] % PS) / PS
    re, im = np.cos(angle) / np.sqrt(PS), -np.sin(angle) / np.sqrt(PS)
    fwd = np.block([[re, im], [-im, re]])
    tables = []
    for full in (fwd, fwd.T):
        high = full.astype(ml_dtypes.bfloat16)
        tables += [high, (full - high.astype(np.float64)).astype(ml_dtypes.bfloat16)]
    return np.stack(tables)


def write_plan(pos_ref, count_ref, plan_ref):
    count = count_ref[0]
    rows = [pos_ref[0, j] for j in range(SLOTS)]
    best_score, best_set = jnp.int32(1 << 30), jnp.int32(0)
    for chosen in range(1 << SLOTS):
        up = down = kept = moved = jnp.int32(0)
        for j in range(SLOTS):
            live = (count > j).astype(jnp.int32)
            if chosen >> j & 1:
                down, moved = down + live * (PS - rows[j]), moved + live
            else:
                up, kept = up + live * rows[j], kept + live
        most = jnp.maximum(up, down)
        score = (
            most
            + jnp.where(jnp.logical_or(up > CAP_KEPT, down > CAP_MOVED), 1 << 20, 0)
            + jnp.where(kept > 2, 1 << 10, 0)
            + jnp.where(moved > 2, 1 << 10, 0)
        )
        better = score < best_score
        best_score = jnp.where(better, score, best_score)
        best_set = jnp.where(better, chosen, best_set)
    for j in range(SLOTS):
        for base in (KEPT, MOVED):
            for field in range(4):
                plan_ref[base + 4 * field + j] = 0
    n = [jnp.int32(0), jnp.int32(0)]
    offset = [jnp.int32(0), jnp.int32(0)]
    spare = PLAN - 16
    for j in range(SLOTS):
        live = count > j
        moved = (best_set >> j) & 1
        for side, base in ((0, KEPT), (1, MOVED)):
            mine = jnp.logical_and(live, moved == side)
            at = jnp.where(mine, base + n[side], spare)
            plan_ref[at] = rows[j]
            plan_ref[at + 4] = pos_ref[1, j]
            plan_ref[at + 8] = offset[side]
            plan_ref[at + 12] = j
            taken = PS - rows[j] if side else rows[j]
            n[side] = n[side] + mine.astype(jnp.int32)
            offset[side] = offset[side] + jnp.where(mine, taken, 0)
    plan_ref[N_KEPT] = n[0]
    plan_ref[N_MOVED] = n[1]


def lanes():
    return lax.broadcasted_iota(jnp.int32, (PS, PS), 1)


def sublanes():
    return lax.broadcasted_iota(jnp.int32, (PS, PS), 0)


def column_blocks(col, width):
    first = pl.multiple_of((col // PS) * PS, PS)
    second = pl.multiple_of(jnp.minimum(first + PS, width - PS), PS)
    return first, second, col % PS


def shifted_columns(left, right, by):
    back = (PS - by) & (PS - 1)
    return jnp.where(lanes() < PS - by, pltpu.roll(left, back, 1), pltpu.roll(right, back, 1))


def read_columns(ref, plane, col):
    first, second, part = column_blocks(col, ref.shape[-1])
    return shifted_columns(ref[plane, :, pl.ds(first, PS)], ref[plane, :, pl.ds(second, PS)], part)


def add_columns(ref, plane, col, value):
    first, second, part = column_blocks(col, ref.shape[-1])
    value = pltpu.roll(value, part, 1)
    here = lanes() >= part
    ref[plane, :, pl.ds(first, PS)] += jnp.where(here, value, 0.0)
    ref[plane, :, pl.ds(second, PS)] += jnp.where(here, 0.0, value)


def entry(plan_ref, base, k):
    return plan_ref[base + k], plan_ref[base + 4 + k], plan_ref[base + 8 + k]


def pack_moved_kernel(pos_ref, count_ref, tile_ref, packed_ref, plan, columns, packed, sems):
    write_plan(pos_ref, count_ref, plan)
    count = plan[N_MOVED]

    def fetch(k):
        start = pl.multiple_of(plan[MOVED + 4 + k] // PS * PS, PS)
        start = pl.multiple_of(jnp.minimum(start, tile_ref.shape[2] - 2 * PS), PS)
        source = tile_ref.at[:, :, pl.ds(start, 2 * PS)]
        return pltpu.make_async_copy(source, columns.at[k], sems.at[k]), start

    for k in range(SLOTS):

        @pl.when(k < count)
        def _(k=k):
            fetch(k)[0].start()

    for k in reversed(range(SLOTS)):

        @pl.when(k < count)
        def _(k=k):
            row, col, offset = entry(plan, MOVED, k)
            copy, start = fetch(k)
            copy.wait()
            for plane in range(PLANES):
                value = shifted_columns(
                    columns[k, plane, :, :PS], columns[k, plane, :, PS:], col - start
                )
                packed[plane, pl.ds(PS + offset - row, PS), :] = value

    packed_ref[...] = packed[:, PS : PS + CAP_MOVED, :]


def pack_moved(positions, counts, tile):
    planes, rows, _ = tile.shape
    smem = pl.BlockSpec(memory_space=pltpu.SMEM)
    return pl.pallas_call(
        pack_moved_kernel,
        out_shape=jax.ShapeDtypeStruct((planes, CAP_MOVED, PS), F32),
        in_specs=[smem, smem, pl.BlockSpec(memory_space=pl.ANY)],
        out_specs=pl.BlockSpec(memory_space=pltpu.VMEM),
        scratch_shapes=[
            pltpu.SMEM((PLAN,), jnp.int32),
            pltpu.VMEM((SLOTS, planes, rows, 2 * PS), F32),
            pltpu.VMEM((planes, CAP_MOVED + 2 * PS, PS), F32),
            pltpu.SemaphoreType.DMA((SLOTS,)),
        ],
        compiler_params=pltpu.CompilerParams(vmem_limit_bytes=PACK_MOVED_VMEM),
        cost_estimate=pl.CostEstimate(flops=0, bytes_accessed=4 * 1024 * 1024, transcendentals=0),
        name="pack_moved",
    )(positions, counts, tile)


def parts_kernel(
    pos_ref, count_ref, pos_above_ref, count_above_ref, tile_ref,
    packed_ref, kept_ref, moved_ref, plan, above, packed,
):
    write_plan(pos_above_ref, count_above_ref, above)

    @pl.loop(0, above[N_KEPT])
    def _(k):
        _, col, offset = entry(above, KEPT, k)
        for plane in range(PLANES):
            packed[plane, pl.ds(offset, PS), :] = read_columns(tile_ref, plane, col)

    packed_ref[...] = packed[:, :CAP_KEPT, :]
    write_plan(pos_ref, count_ref, plan)

    @pl.loop(0, plan[N_KEPT])
    def _(k):
        for plane in range(PLANES):
            kept_ref[k, plane] = read_columns(tile_ref, plane, plan[KEPT + 4 + k])

    @pl.loop(0, above[N_MOVED])
    def _(k):
        for plane in range(PLANES):
            moved_ref[k, plane] = read_columns(tile_ref, plane, above[MOVED + 4 + k])


def parts(where, tile):
    planes = tile.shape[0]
    smem = pl.BlockSpec(memory_space=pltpu.SMEM)
    vmem = pl.BlockSpec(memory_space=pltpu.VMEM)
    windows = jax.ShapeDtypeStruct((SLOTS, planes, PS, PS), F32)
    numbers = jax.ShapeDtypeStruct((PLAN,), jnp.int32)
    return pl.pallas_call(
        parts_kernel,
        out_shape=(
            jax.ShapeDtypeStruct((planes, CAP_KEPT, PS), F32), windows, windows, numbers, numbers
        ),
        in_specs=[smem] * 4 + [vmem],
        out_specs=(vmem, vmem, vmem, smem, smem),
        scratch_shapes=[pltpu.VMEM((planes, CAP_KEPT + PS, PS), F32)],
        compiler_params=pltpu.CompilerParams(vmem_limit_bytes=PACK_VMEM),
        cost_estimate=pl.CostEstimate(flops=0, bytes_accessed=8 * 1024 * 1024, transcendentals=0),
        name="parts",
    )(*where, tile)


def split(x):
    high = x.astype(jnp.bfloat16)
    return high, (x - high.astype(F32)).astype(jnp.bfloat16)


def dot(a, b):
    return jnp.dot(a, b, preferred_element_type=F32)


def times_table(x, table):
    high, low = split(x)
    return dot(low, table[0]) + dot(high, table[1]) + dot(high, table[0])


def turned(x):
    return jnp.concatenate([x[:, :PS].T, x[:, PS:].T], axis=1)


def halves(x):
    return x[:, :PS], x[:, PS:]


def times(a, b):
    (a_re, a_im), (b_re, b_im) = a, b
    return jnp.concatenate([a_re * b_re - a_im * b_im, a_re * b_im + a_im * b_re], axis=1)


def times_conj(a, b):
    (a_re, a_im), (b_re, b_im) = a, b
    return jnp.concatenate([a_re * b_re + a_im * b_im, a_im * b_re - a_re * b_im], axis=1)


def wave_kernel(
    moved, plan_ref, own_ref, msg_ref, pattern_ref, probe_ref, prop_ref, table_ref,
    *refs,
):
    grads_ref, out_ref, msg, patch, grad, waves, packed = refs[-7:]
    cap = msg_ref.shape[1]
    msg[:, :cap, :] = msg_ref[...]
    base = MOVED if moved else KEPT
    count = plan_ref[N_MOVED if moved else N_KEPT]
    layers = PLANES // 2
    chains = range(patch.shape[0])
    fwd = (table_ref[0], table_ref[1])
    bwd = (table_ref[2], table_ref[3])

    def transform(xs, table):
        return [times_table(turned(times_table(x, table)), table) for x in xs]

    def propagate(xs, product):
        prop = (prop_ref[0], prop_ref[1])
        xs = [product(halves(x), prop) for x in transform(xs, fwd)]
        return transform(xs, bwd)

    def layer_of(i, layer):
        return patch[i, 2 * layer, PS : 2 * PS, :], patch[i, 2 * layer + 1, PS : 2 * PS, :]

    @pl.loop(0, (count + len(chains) - 1) // len(chains))
    def _(group):
        first = group * len(chains)
        for i in chains:

            @pl.when(first + i < count)
            def _(i=i, k=first + i):
                row, _, offset = entry(plan_ref, base, k)
                for plane in range(PLANES):
                    own, other = own_ref[k, plane], msg[plane, pl.ds(offset, PS), :]
                    if moved:
                        patch[i, plane, PS : 2 * PS, :] = other
                        patch[i, plane, pl.ds(2 * PS - row, PS), :] = own
                    else:
                        patch[i, plane, pl.ds(PS - row, PS), :] = own
                        patch[i, plane, pl.ds(2 * PS - row, PS), :] = other

        probe = (probe_ref[0], probe_ref[1])
        for layer in range(layers):
            xs = []
            for i in chains:
                wave = halves(waves[layer, i]) if layer else probe
                xs.append(times(wave, layer_of(i, layer)))
            if layer + 1 < layers:
                for i, x in enumerate(propagate(xs, times)):
                    waves[layer + 1, i] = x
        xs = transform(xs, fwd)
        for i in chains:
            slot = plan_ref[base + 12 + jnp.minimum(first + i, SLOTS - 1)]
            re, im = halves(xs[i])
            scale = 4.0 * (re * re + im * im - pattern_ref[slot].T)
            xs[i] = jnp.concatenate([scale * re, scale * im], axis=1)
        xs = transform(xs, bwd)
        for layer in reversed(range(layers)):
            for i in chains:
                wave = halves(waves[layer, i]) if layer else probe
                d_re, d_im = halves(times_conj(halves(xs[i]), wave))
                grad[i, 2 * layer, :PS, :] = d_re
                grad[i, 2 * layer + 1, :PS, :] = d_im
                if layer:
                    xs[i] = times_conj(halves(xs[i]), layer_of(i, layer))
            if layer:
                xs = propagate(xs, times_conj)

        for i in chains:

            @pl.when(first + i < count)
            def _(i=i, k=first + i):
                row, _, offset = entry(plan_ref, base, k)
                grads_ref[k] = grad[i, :, :PS, :]
                for plane in range(PLANES):
                    start = 0 if moved else PS - row
                    packed[plane, pl.ds(offset, PS), :] = grad[i, plane, pl.ds(start, PS), :]

    out_ref[...] = packed[:, :cap, :]


def gradients(moved, plan, own, msg, patterns, probe, prop, tables, after=()):
    planes = own.shape[1]
    smem = pl.BlockSpec(memory_space=pltpu.SMEM)
    vmem = pl.BlockSpec(memory_space=pltpu.VMEM)
    return pl.pallas_call(
        functools.partial(wave_kernel, moved),
        out_shape=(
            jax.ShapeDtypeStruct((SLOTS, planes, PS, PS), F32),
            jax.ShapeDtypeStruct(msg.shape, F32),
        ),
        in_specs=[smem] + [vmem] * 6 + [pl.BlockSpec(memory_space=pl.ANY)] * len(after),
        out_specs=(vmem, vmem),
        scratch_shapes=[
            pltpu.VMEM((planes, msg.shape[1] + PS, PS), F32),
            pltpu.VMEM((CHAINS, planes, 3 * PS, PS), F32),
            pltpu.VMEM((CHAINS, planes, 2 * PS, PS), F32),
            pltpu.VMEM((planes // 2, CHAINS, PS, 2 * PS), F32),
            pltpu.VMEM((planes, msg.shape[1] + PS, PS), F32),
        ],
        compiler_params=pltpu.CompilerParams(vmem_limit_bytes=WAVE_VMEM),
        cost_estimate=pl.CostEstimate(
            flops=6 * 1024**3, bytes_accessed=8 * 1024 * 1024, transcendentals=0
        ),
        name="waves_moved" if moved else "waves_kept",
    )(plan, own, msg, patterns, probe, prop, tables, *after)


def deposit_kernel(
    plan, above, kept_ref, moved_ref, below_ref, out_ref, shift
):
    out_ref[...] = jnp.zeros_like(out_ref)

    @pl.loop(0, plan[N_KEPT])
    def _(k):
        row, col, _ = entry(plan, KEPT, k)
        inside = sublanes() >= row
        for plane in range(PLANES):
            shift[plane, pl.ds(row, PS), :] = kept_ref[k, plane]
            add_columns(out_ref, plane, col, jnp.where(inside, shift[plane, :PS, :], 0.0))

    @pl.loop(0, above[N_MOVED])
    def _(k):
        row, col, _ = entry(above, MOVED, k)
        inside = sublanes() < row
        for plane in range(PLANES):
            shift[plane, pl.ds(row, PS), :] = moved_ref[k, plane]
            add_columns(out_ref, plane, col, jnp.where(inside, shift[plane, PS : 2 * PS, :], 0.0))

    shift[:, PS : PS + CAP_MOVED, :] = below_ref[...]

    @pl.loop(0, plan[N_MOVED])
    def _(k):
        row, col, offset = entry(plan, MOVED, k)
        inside = sublanes() >= row
        for plane in range(PLANES):
            value = shift[plane, pl.ds(PS + offset - row, PS), :]
            add_columns(out_ref, plane, col, jnp.where(inside, value, 0.0))


def deposit(plans, kept, moved, from_below, shape):
    planes = shape[0]
    smem = pl.BlockSpec(memory_space=pltpu.SMEM)
    vmem = pl.BlockSpec(memory_space=pltpu.VMEM)
    return pl.pallas_call(
        deposit_kernel,
        out_shape=jax.ShapeDtypeStruct(shape, F32),
        in_specs=[smem] * 2 + [vmem] * 3,
        out_specs=vmem,
        scratch_shapes=[pltpu.VMEM((planes, CAP_MOVED + 2 * PS, PS), F32)],
        compiler_params=pltpu.CompilerParams(vmem_limit_bytes=PACK_VMEM),
        cost_estimate=pl.CostEstimate(flops=0, bytes_accessed=4 * 1024 * 1024, transcendentals=0),
        name="deposit",
    )(*plans, kept, moved, from_below)


def finish_kernel(plan, sum_ref, msg_ref, out_ref, total, msg, sems):
    msg[:, :CAP_KEPT, :] = msg_ref[...]
    copies = []
    for plane in range(PLANES):
        total[plane] = sum_ref[plane]

        @pl.loop(0, plan[N_KEPT])
        def _(k, plane=plane):
            row, col, offset = entry(plan, KEPT, k)
            value = jnp.where(sublanes() < row, msg[plane, pl.ds(offset, PS), :], 0.0)
            add_columns(total, plane, col, value)

        copy = pltpu.make_async_copy(total.at[plane], out_ref.at[plane], sems.at[plane])
        copy.start()
        copies.append(copy)
    for copy in copies:
        copy.wait()


def finish(above, summed, from_above):
    planes = summed.shape[0]
    smem = pl.BlockSpec(memory_space=pltpu.SMEM)
    vmem = pl.BlockSpec(memory_space=pltpu.VMEM)
    return pl.pallas_call(
        finish_kernel,
        out_shape=jax.ShapeDtypeStruct(summed.shape, F32),
        in_specs=[smem, vmem, vmem],
        out_specs=pl.BlockSpec(memory_space=pl.ANY),
        scratch_shapes=[
            pltpu.VMEM(summed.shape, F32),
            pltpu.VMEM((planes, CAP_KEPT + PS, PS), F32),
            pltpu.SemaphoreType.DMA((planes,)),
        ],
        compiler_params=pltpu.CompilerParams(vmem_limit_bytes=PACK_VMEM),
        cost_estimate=pl.CostEstimate(flops=0, bytes_accessed=4 * 1024 * 1024, transcendentals=0),
        name="finish",
    )(above, summed, from_above)


def per_device(tile_object, probe_wave, propagator_phase, diffraction, positions, counts):
    layers, two, rows, width = tile_object.shape
    tile = tile_object.reshape(layers * two, rows, width)
    positions = positions.T
    positions_above = shifted(positions, "ty", 1)
    counts_above = shifted(counts, "ty", 1)
    patterns_above = shifted(diffraction, "ty", 1)
    phase = propagator_phase.T
    prop = jnp.stack([jnp.cos(phase), jnp.sin(phase)])
    tables = jnp.asarray(dft_tables())

    down = pack_moved(positions, counts, tile)
    down, positions_above, counts_above, patterns_above = lax.optimization_barrier(
        (down, positions_above, counts_above, patterns_above)
    )
    rows_above = shifted(down, "ty", 1)
    where = (positions, counts, positions_above, counts_above)
    up, own_kept, own_moved, plan, above = parts(where, tile)
    up, rows_above = lax.optimization_barrier((up, rows_above))
    rows_below = shifted(up, "ty", -1)
    moved, back_up = gradients(
        True, above, own_moved, rows_above, patterns_above,
        probe_wave, prop, tables,
    )
    from_below = shifted(back_up, "ty", -1)
    kept, back_down = gradients(
        False, plan, own_kept, rows_below, diffraction,
        probe_wave, prop, tables, after=(moved,),
    )
    from_above = shifted(back_down, "ty", 1)
    summed = deposit((plan, above), kept, moved, from_below, tile.shape)
    out = finish(above, summed, from_above)
    return out.reshape(tile_object.shape)


def solution(mesh):
    in_specs = (
        P(None, None, ("grp", "ty"), None),
        P(),
        P(),
        P(("grp", "ty"), None, None),
        P(("grp", "ty"), None),
        P(("grp", "ty")),
    )
    out_specs = P(None, None, ("grp", "ty"), None)
    return jax.shard_map(
        per_device, mesh=mesh, in_specs=in_specs, out_specs=out_specs, check_vma=False
    )
```

```python
import functools

import jax
import jax.numpy as jnp
import ml_dtypes
import numpy as np
from jax import lax
from jax.experimental import pallas as pl
from jax.experimental.pallas import tpu as pltpu
from jax.sharding import PartitionSpec as P

PS = 128
PLANES = 8
SLOTS = 4
CAP_KEPT, CAP_MOVED = 152, 160
F32 = jnp.float32

N_KEPT, N_MOVED = 0, 1
KEPT, MOVED = 2, 18
PLAN = 128

CHAINS = 3
PACK_VMEM = 8 * 1024 * 1024
PACK_MOVED_VMEM = 60 * 1024 * 1024
WAVE_VMEM = 20 * 1024 * 1024


def shifted(x, axis, by):
    peers = lax.axis_size(axis)
    return lax.ppermute(x, axis, [(i, (i + by) % peers) for i in range(peers)])


def dft_tables():
    index = np.arange(PS)
    angle = 2.0 * np.pi * (index[:, None] * index[None, :] % PS) / PS
    re, im = np.cos(angle) / np.sqrt(PS), -np.sin(angle) / np.sqrt(PS)
    fwd = np.block([[re, im], [-im, re]])
    tables = []
    for full in (fwd, fwd.T):
        high = full.astype(ml_dtypes.bfloat16)
        tables += [high, (full - high.astype(np.float64)).astype(ml_dtypes.bfloat16)]
    return np.stack(tables)


def write_plan(pos_ref, count_ref, plan_ref):
    count = count_ref[0]
    rows = [pos_ref[0, j] for j in range(SLOTS)]
    best_score, best_set = jnp.int32(1 << 30), jnp.int32(0)
    for chosen in range(1 << SLOTS):
        up = down = kept = moved = jnp.int32(0)
        for j in range(SLOTS):
            live = (count > j).astype(jnp.int32)
            if chosen >> j & 1:
                down, moved = down + live * (PS - rows[j]), moved + live
            else:
                up, kept = up + live * rows[j], kept + live
        most = jnp.maximum(up, down)
        score = (
            most
            + jnp.where(jnp.logical_or(up > CAP_KEPT, down > CAP_MOVED), 1 << 20, 0)
            + jnp.where(kept > 2, 1 << 10, 0)
            + jnp.where(moved > 2, 1 << 10, 0)
        )
        better = score < best_score
        best_score = jnp.where(better, score, best_score)
        best_set = jnp.where(better, chosen, best_set)
    for j in range(SLOTS):
        for base in (KEPT, MOVED):
            for field in range(4):
                plan_ref[base + 4 * field + j] = 0
    n = [jnp.int32(0), jnp.int32(0)]
    offset = [jnp.int32(0), jnp.int32(0)]
    spare = PLAN - 16
    for j in range(SLOTS):
        live = count > j
        moved = (best_set >> j) & 1
        for side, base in ((0, KEPT), (1, MOVED)):
            mine = jnp.logical_and(live, moved == side)
            at = jnp.where(mine, base + n[side], spare)
            plan_ref[at] = rows[j]
            plan_ref[at + 4] = pos_ref[1, j]
            plan_ref[at + 8] = offset[side]
            plan_ref[at + 12] = j
            taken = PS - rows[j] if side else rows[j]
            n[side] = n[side] + mine.astype(jnp.int32)
            offset[side] = offset[side] + jnp.where(mine, taken, 0)
    plan_ref[N_KEPT] = n[0]
    plan_ref[N_MOVED] = n[1]


def lanes():
    return lax.broadcasted_iota(jnp.int32, (PS, PS), 1)


def sublanes():
    return lax.broadcasted_iota(jnp.int32, (PS, PS), 0)


def column_blocks(col, width):
    first = pl.multiple_of((col // PS) * PS, PS)
    second = pl.multiple_of(jnp.minimum(first + PS, width - PS), PS)
    return first, second, col % PS


def shifted_columns(left, right, by):
    back = (PS - by) & (PS - 1)
    return jnp.where(lanes() < PS - by, pltpu.roll(left, back, 1), pltpu.roll(right, back, 1))


def read_columns(ref, plane, col):
    first, second, part = column_blocks(col, ref.shape[-1])
    return shifted_columns(ref[plane, :, pl.ds(first, PS)], ref[plane, :, pl.ds(second, PS)], part)


def add_columns(ref, plane, col, value):
    first, second, part = column_blocks(col, ref.shape[-1])
    value = pltpu.roll(value, part, 1)
    here = lanes() >= part
    ref[plane, :, pl.ds(first, PS)] += jnp.where(here, value, 0.0)
    ref[plane, :, pl.ds(second, PS)] += jnp.where(here, 0.0, value)


def entry(plan_ref, base, k):
    return plan_ref[base + k], plan_ref[base + 4 + k], plan_ref[base + 8 + k]


def pack_moved_kernel(pos_ref, count_ref, tile_ref, packed_ref, plan, columns, packed, sems):
    write_plan(pos_ref, count_ref, plan)
    count = plan[N_MOVED]

    def fetch(k):
        start = pl.multiple_of(plan[MOVED + 4 + k] // PS * PS, PS)
        start = pl.multiple_of(jnp.minimum(start, tile_ref.shape[2] - 2 * PS), PS)
        source = tile_ref.at[:, :, pl.ds(start, 2 * PS)]
        return pltpu.make_async_copy(source, columns.at[k], sems.at[k]), start

    for k in range(SLOTS):

        @pl.when(k < count)
        def _(k=k):
            fetch(k)[0].start()

    for k in reversed(range(SLOTS)):

        @pl.when(k < count)
        def _(k=k):
            row, col, offset = entry(plan, MOVED, k)
            copy, start = fetch(k)
            copy.wait()
            for plane in range(PLANES):
                value = shifted_columns(
                    columns[k, plane, :, :PS], columns[k, plane, :, PS:], col - start
                )
                packed[plane, pl.ds(PS + offset - row, PS), :] = value

    packed_ref[...] = packed[:, PS : PS + CAP_MOVED, :]


def pack_moved(positions, counts, tile):
    planes, rows, _ = tile.shape
    smem = pl.BlockSpec(memory_space=pltpu.SMEM)
    return pl.pallas_call(
        pack_moved_kernel,
        out_shape=jax.ShapeDtypeStruct((planes, CAP_MOVED, PS), F32),
        in_specs=[smem, smem, pl.BlockSpec(memory_space=pl.ANY)],
        out_specs=pl.BlockSpec(memory_space=pltpu.VMEM),
        scratch_shapes=[
            pltpu.SMEM((PLAN,), jnp.int32),
            pltpu.VMEM((SLOTS, planes, rows, 2 * PS), F32),
            pltpu.VMEM((planes, CAP_MOVED + 2 * PS, PS), F32),
            pltpu.SemaphoreType.DMA((SLOTS,)),
        ],
        compiler_params=pltpu.CompilerParams(vmem_limit_bytes=PACK_MOVED_VMEM),
        cost_estimate=pl.CostEstimate(flops=0, bytes_accessed=4 * 1024 * 1024, transcendentals=0),
        name="pack_moved",
    )(positions, counts, tile)


def parts_kernel(
    pos_ref, count_ref, pos_above_ref, count_above_ref, tile_ref,
    packed_ref, kept_ref, moved_ref, plan, above, packed,
):
    write_plan(pos_above_ref, count_above_ref, above)

    @pl.loop(0, above[N_KEPT])
    def _(k):
        _, col, offset = entry(above, KEPT, k)
        for plane in range(PLANES):
            packed[plane, pl.ds(offset, PS), :] = read_columns(tile_ref, plane, col)

    packed_ref[...] = packed[:, :CAP_KEPT, :]
    write_plan(pos_ref, count_ref, plan)

    @pl.loop(0, plan[N_KEPT])
    def _(k):
        for plane in range(PLANES):
            kept_ref[k, plane] = read_columns(tile_ref, plane, plan[KEPT + 4 + k])

    @pl.loop(0, above[N_MOVED])
    def _(k):
        for plane in range(PLANES):
            moved_ref[k, plane] = read_columns(tile_ref, plane, above[MOVED + 4 + k])


def parts(where, tile):
    planes = tile.shape[0]
    smem = pl.BlockSpec(memory_space=pltpu.SMEM)
    vmem = pl.BlockSpec(memory_space=pltpu.VMEM)
    windows = jax.ShapeDtypeStruct((SLOTS, planes, PS, PS), F32)
    numbers = jax.ShapeDtypeStruct((PLAN,), jnp.int32)
    return pl.pallas_call(
        parts_kernel,
        out_shape=(
            jax.ShapeDtypeStruct((planes, CAP_KEPT, PS), F32), windows, windows, numbers, numbers
        ),
        in_specs=[smem] * 4 + [vmem],
        out_specs=(vmem, vmem, vmem, smem, smem),
        scratch_shapes=[pltpu.VMEM((planes, CAP_KEPT + PS, PS), F32)],
        compiler_params=pltpu.CompilerParams(vmem_limit_bytes=PACK_VMEM),
        cost_estimate=pl.CostEstimate(flops=0, bytes_accessed=8 * 1024 * 1024, transcendentals=0),
        name="parts",
    )(*where, tile)


def split(x):
    high = x.astype(jnp.bfloat16)
    return high, (x - high.astype(F32)).astype(jnp.bfloat16)


def dot(a, b):
    return jnp.dot(a, b, preferred_element_type=F32)


def times_table(x, table):
    high, low = split(x)
    return dot(low, table[0]) + dot(high, table[1]) + dot(high, table[0])


def turned(x):
    return jnp.concatenate([x[:, :PS].T, x[:, PS:].T], axis=1)


def halves(x):
    return x[:, :PS], x[:, PS:]


def times(a, b):
    (a_re, a_im), (b_re, b_im) = a, b
    return jnp.concatenate([a_re * b_re - a_im * b_im, a_re * b_im + a_im * b_re], axis=1)


def times_conj(a, b):
    (a_re, a_im), (b_re, b_im) = a, b
    return jnp.concatenate([a_re * b_re + a_im * b_im, a_im * b_re - a_re * b_im], axis=1)


def wave_kernel(
    moved, plan_ref, own_ref, msg_ref, pattern_ref, probe_ref, prop_ref, table_ref,
    *refs,
):
    grads_ref, out_ref, msg, patch, grad, waves, packed = refs[-7:]
    cap = msg_ref.shape[1]
    msg[:, :cap, :] = msg_ref[...]
    base = MOVED if moved else KEPT
    count = plan_ref[N_MOVED if moved else N_KEPT]
    layers = PLANES // 2
    chains = range(patch.shape[0])
    fwd = (table_ref[0], table_ref[1])
    bwd = (table_ref[2], table_ref[3])

    def transform(xs, table):
        return [times_table(turned(times_table(x, table)), table) for x in xs]

    def propagate(xs, product):
        prop = (prop_ref[0], prop_ref[1])
        xs = [product(halves(x), prop) for x in transform(xs, fwd)]
        return transform(xs, bwd)

    def layer_of(i, layer):
        return patch[i, 2 * layer, PS : 2 * PS, :], patch[i, 2 * layer + 1, PS : 2 * PS, :]

    @pl.loop(0, (count + len(chains) - 1) // len(chains))
    def _(group):
        first = group * len(chains)
        for i in chains:

            @pl.when(first + i < count)
            def _(i=i, k=first + i):
                row, _, offset = entry(plan_ref, base, k)
                for plane in range(PLANES):
                    own, other = own_ref[k, plane], msg[plane, pl.ds(offset, PS), :]
                    if moved:
                        patch[i, plane, PS : 2 * PS, :] = other
                        patch[i, plane, pl.ds(2 * PS - row, PS), :] = own
                    else:
                        patch[i, plane, pl.ds(PS - row, PS), :] = own
                        patch[i, plane, pl.ds(2 * PS - row, PS), :] = other

        probe = (probe_ref[0], probe_ref[1])
        for layer in range(layers):
            xs = []
            for i in chains:
                wave = halves(waves[layer, i]) if layer else probe
                xs.append(times(wave, layer_of(i, layer)))
            if layer + 1 < layers:
                for i, x in enumerate(propagate(xs, times)):
                    waves[layer + 1, i] = x
        xs = transform(xs, fwd)
        for i in chains:
            slot = plan_ref[base + 12 + jnp.minimum(first + i, SLOTS - 1)]
            re, im = halves(xs[i])
            scale = 4.0 * (re * re + im * im - pattern_ref[slot].T)
            xs[i] = jnp.concatenate([scale * re, scale * im], axis=1)
        xs = transform(xs, bwd)
        for layer in reversed(range(layers)):
            for i in chains:
                wave = halves(waves[layer, i]) if layer else probe
                d_re, d_im = halves(times_conj(halves(xs[i]), wave))
                grad[i, 2 * layer, :PS, :] = d_re
                grad[i, 2 * layer + 1, :PS, :] = d_im
                if layer:
                    xs[i] = times_conj(halves(xs[i]), layer_of(i, layer))
            if layer:
                xs = propagate(xs, times_conj)

        for i in chains:

            @pl.when(first + i < count)
            def _(i=i, k=first + i):
                row, _, offset = entry(plan_ref, base, k)
                grads_ref[k] = grad[i, :, :PS, :]
                for plane in range(PLANES):
                    start = 0 if moved else PS - row
                    packed[plane, pl.ds(offset, PS), :] = grad[i, plane, pl.ds(start, PS), :]

    out_ref[...] = packed[:, :cap, :]


def gradients(moved, plan, own, msg, patterns, probe, prop, tables, after=()):
    planes = own.shape[1]
    smem = pl.BlockSpec(memory_space=pltpu.SMEM)
    vmem = pl.BlockSpec(memory_space=pltpu.VMEM)
    return pl.pallas_call(
        functools.partial(wave_kernel, moved),
        out_shape=(
            jax.ShapeDtypeStruct((SLOTS, planes, PS, PS), F32),
            jax.ShapeDtypeStruct(msg.shape, F32),
        ),
        in_specs=[smem] + [vmem] * 6 + [pl.BlockSpec(memory_space=pl.ANY)] * len(after),
        out_specs=(vmem, vmem),
        scratch_shapes=[
            pltpu.VMEM((planes, msg.shape[1] + PS, PS), F32),
            pltpu.VMEM((CHAINS, planes, 3 * PS, PS), F32),
            pltpu.VMEM((CHAINS, planes, 2 * PS, PS), F32),
            pltpu.VMEM((planes // 2, CHAINS, PS, 2 * PS), F32),
            pltpu.VMEM((planes, msg.shape[1] + PS, PS), F32),
        ],
        compiler_params=pltpu.CompilerParams(vmem_limit_bytes=WAVE_VMEM),
        cost_estimate=pl.CostEstimate(
            flops=6 * 1024**3, bytes_accessed=8 * 1024 * 1024, transcendentals=0
        ),
        name="waves_moved" if moved else "waves_kept",
    )(plan, own, msg, patterns, probe, prop, tables, *after)


def deposit_kernel(
    plan, above, kept_ref, moved_ref, below_ref, out_ref, shift
):
    out_ref[...] = jnp.zeros_like(out_ref)

    @pl.loop(0, plan[N_KEPT])
    def _(k):
        row, col, _ = entry(plan, KEPT, k)
        inside = sublanes() >= row
        for plane in range(PLANES):
            shift[plane, pl.ds(row, PS), :] = kept_ref[k, plane]
            add_columns(out_ref, plane, col, jnp.where(inside, shift[plane, :PS, :], 0.0))

    @pl.loop(0, above[N_MOVED])
    def _(k):
        row, col, _ = entry(above, MOVED, k)
        inside = sublanes() < row
        for plane in range(PLANES):
            shift[plane, pl.ds(row, PS), :] = moved_ref[k, plane]
            add_columns(out_ref, plane, col, jnp.where(inside, shift[plane, PS : 2 * PS, :], 0.0))

    shift[:, PS : PS + CAP_MOVED, :] = below_ref[...]

    @pl.loop(0, plan[N_MOVED])
    def _(k):
        row, col, offset = entry(plan, MOVED, k)
        inside = sublanes() >= row
        for plane in range(PLANES):
            value = shift[plane, pl.ds(PS + offset - row, PS), :]
            add_columns(out_ref, plane, col, jnp.where(inside, value, 0.0))


def deposit(plans, kept, moved, from_below, shape):
    planes = shape[0]
    smem = pl.BlockSpec(memory_space=pltpu.SMEM)
    vmem = pl.BlockSpec(memory_space=pltpu.VMEM)
    return pl.pallas_call(
        deposit_kernel,
        out_shape=jax.ShapeDtypeStruct(shape, F32),
        in_specs=[smem] * 2 + [vmem] * 3,
        out_specs=vmem,
        scratch_shapes=[pltpu.VMEM((planes, CAP_MOVED + 2 * PS, PS), F32)],
        compiler_params=pltpu.CompilerParams(vmem_limit_bytes=PACK_VMEM),
        cost_estimate=pl.CostEstimate(flops=0, bytes_accessed=4 * 1024 * 1024, transcendentals=0),
        name="deposit",
    )(*plans, kept, moved, from_below)


def finish_kernel(plan, sum_ref, msg_ref, out_ref, total, msg, sems):
    msg[:, :CAP_KEPT, :] = msg_ref[...]
    copies = []
    for plane in range(PLANES):
        total[plane] = sum_ref[plane]

        @pl.loop(0, plan[N_KEPT])
        def _(k, plane=plane):
            row, col, offset = entry(plan, KEPT, k)
            value = jnp.where(sublanes() < row, msg[plane, pl.ds(offset, PS), :], 0.0)
            add_columns(total, plane, col, value)

        copy = pltpu.make_async_copy(total.at[plane], out_ref.at[plane], sems.at[plane])
        copy.start()
        copies.append(copy)
    for copy in copies:
        copy.wait()


def finish(above, summed, from_above):
    planes = summed.shape[0]
    smem = pl.BlockSpec(memory_space=pltpu.SMEM)
    vmem = pl.BlockSpec(memory_space=pltpu.VMEM)
    return pl.pallas_call(
        finish_kernel,
        out_shape=jax.ShapeDtypeStruct(summed.shape, F32),
        in_specs=[smem, vmem, vmem],
        out_specs=pl.BlockSpec(memory_space=pl.ANY),
        scratch_shapes=[
            pltpu.VMEM(summed.shape, F32),
            pltpu.VMEM((planes, CAP_KEPT + PS, PS), F32),
            pltpu.SemaphoreType.DMA((planes,)),
        ],
        compiler_params=pltpu.CompilerParams(vmem_limit_bytes=PACK_VMEM),
        cost_estimate=pl.CostEstimate(flops=0, bytes_accessed=4 * 1024 * 1024, transcendentals=0),
        name="finish",
    )(above, summed, from_above)


def per_device(tile_object, probe_wave, propagator_phase, diffraction, positions, counts):
    layers, two, rows, width = tile_object.shape
    tile = tile_object.reshape(layers * two, rows, width)
    positions = positions.T
    positions_above = shifted(positions, "ty", 1)
    counts_above = shifted(counts, "ty", 1)
    patterns_above = shifted(diffraction, "ty", 1)
    phase = propagator_phase.T
    prop = jnp.stack([jnp.cos(phase), jnp.sin(phase)])
    tables = jnp.asarray(dft_tables())

    down = pack_moved(positions, counts, tile)
    down, positions_above, counts_above, patterns_above = lax.optimization_barrier(
        (down, positions_above, counts_above, patterns_above)
    )
    rows_above = shifted(down, "ty", 1)
    where = (positions, counts, positions_above, counts_above)
    up, own_kept, own_moved, plan, above = parts(where, tile)
    up, rows_above = lax.optimization_barrier((up, rows_above))
    rows_below = shifted(up, "ty", -1)
    moved, back_up = gradients(
        True, above, own_moved, rows_above, patterns_above,
        probe_wave, prop, tables,
    )
    from_below = shifted(back_up, "ty", -1)
    kept, back_down = gradients(
        False, plan, own_kept, rows_below, diffraction,
        probe_wave, prop, tables, after=(moved,),
    )
    from_above = shifted(back_down, "ty", 1)
    summed = deposit((plan, above), kept, moved, from_below, tile.shape)
    out = finish(above, summed, from_above)
    return out.reshape(tile_object.shape)


def solution(mesh):
    in_specs = (
        P(None, None, ("grp", "ty"), None),
        P(),
        P(),
        P(("grp", "ty"), None, None),
        P(("grp", "ty"), None),
        P(("grp", "ty")),
    )
    out_specs = P(None, None, ("grp", "ty"), None)
    return jax.shard_map(
        per_device, mesh=mesh, in_specs=in_specs, out_specs=out_specs, check_vma=False
    )
```
